256 devices in a mesh: sample: 4 (over y_lo, core), row: 16 (over z, y_hi), col: 4 (over x).
Axes of the slice: x: 4, y: 4 (y_hi: 2, y_lo: 2; y = y_hi * 2 + y_lo), z: 8, core: 2. Of those that a mesh axis runs over, the one named last changes fastest.
Arguments:
- trunk_pair: bfloat16 [1024, 1024, 128], P('row', 'col'), may hold values from -6 to 6
- distance_bins: int32 [4, 1024, 1024], P('sample', 'row', 'col'), may hold values from 0 to 38
- token_mask: int32 [1024], replicated, may hold values 0 or 1
- single: bfloat16 [1024, 384], P('row', 'sample'), may hold values from -6 to 6
- dist_weight: bfloat16 [39, 128], replicated, may hold values from -5 to 5
- pair_gain: float32 [128], replicated, may hold values from 0.1 to 1.9
- bias_weight: bfloat16 [128, 16], replicated
- single_gain: float32 [384], replicated, may hold values from 0.1 to 1.9
- query_weight: bfloat16 [384, 384], P(None, 'col'), may hold values from -0.3125 to 0.3125
- query_bias: float32 [384], P('col'), may hold values from -3 to 3
- key_weight: bfloat16 [384, 384], P(None, 'col'), may hold values from -0.3125 to 0.3125
- value_weight: bfloat16 [384, 384], P(None, 'col'), may hold values from -0.3125 to 0.3125
- gate_weight: bfloat16 [384, 384], P(None, 'col'), may hold values from -0.3125 to 0.3125
- out_weight: bfloat16 [384, 384], P('col'), may hold values from -0.3125 to 0.3125
Outputs:
- single_update: bfloat16 [4, 1024, 384], P('sample', 'row', 'col')
The draws below stay inside these ranges and needn't reach their ends.
All inputs are finite; a program needn't handle non-finite values.
Results may differ from the reference program's by a relative error of at most 0.015.
The reference program's roundings to bfloat16 on the way (of `pair_normed`, `pair_bias`, `single_normed`, `probs` and `gated`) count: a program that leaves them out, or rounds other values in their place, can miss the bound.
Values may be sent and summed in bfloat16 or wider, within the bound.
No kernel may reach another device: no remote copies, remote signals or barrier semaphores. Data moves between devices by JAX's collectives and lax.ppermute only.
A program may use at most 64 MiB of HBM per device.

```python
import jax
import jax.numpy as jnp
from jax import lax

CZ = 128
CS = 384
HEADS = 16
BINS = 39
TOKENS = 1024
SAMPLES = 4


def draw_bias_weight(key, part):
    key = jax.random.fold_in(key, 5)
    normal_part = jax.random.normal(key, (CZ, HEADS), jnp.float32)
    return (normal_part * 0.09).astype(jnp.bfloat16)


def with_ends(entries, own_key, least, top_value):
    extent = entries.shape
    index_at = [jax.random.randint(jax.random.fold_in(own_key, axis), (), 0, extent[axis]) for axis in range(len(extent))]
    entries = entries.at[tuple(index_at)].set(least)
    longest = extent.index(max(extent))
    index_at[longest] = (index_at[longest] + 1) % extent[longest]
    return entries.at[tuple(index_at)].set(top_value)


def shard_levels(key, extent, split, least, top_value):
    loudness, own = 1.0, jax.random.fold_in(key, 6)
    for dim, blocks in split:
        steps = jnp.exp(jax.random.uniform(jax.random.fold_in(own, dim), (blocks,), jnp.float32, least / len(split), top_value / len(split)))
        loudness = loudness * jnp.repeat(steps, extent[dim] // blocks).reshape([-1 if axis == dim else 1 for axis in range(len(extent))])
    return loudness


def bell_draw(key, dims, width, limit, pieces=(), kind=jnp.bfloat16):
    entries = width * jax.random.normal(key, dims, jnp.float32)
    if pieces:
        entries = entries * shard_levels(key, dims, pieces, -0.22, 0.18)
    return jnp.clip(entries, -limit, limit).astype(kind)


def setup_inputs(seed: int = 0) -> dict:
    splits = jax.random.split(jax.random.key(seed), 15)
    trunk_pair = bell_draw(splits[0], (TOKENS, TOKENS, CZ), 1.0, 6.0, ((0, 16), (1, 4)))
    distance_bins = with_ends(jax.random.randint(splits[1], (SAMPLES, TOKENS, TOKENS), 0, BINS), jax.random.fold_in(splits[1], 1), 0, BINS - 1).astype(jnp.int32)
    token_mask = with_ends((jax.random.randint(splits[2], (TOKENS,), 0, 8) < 7).astype(jnp.int32), jax.random.fold_in(splits[2], 1), 0, 1)
    single = bell_draw(splits[3], (TOKENS, CS), 1.0, 6.0, ((0, 16), (1, 4)))
    dist_weight = bell_draw(splits[4], (BINS, CZ), 1.0, 5.0)
    pair_gain = jnp.clip(1.0 + 0.18 * jax.random.normal(splits[5], (CZ,), jnp.float32), 0.1, 1.9)
    bias_weight = draw_bias_weight(jax.random.fold_in(splits[14], 71), 0)
    single_gain = jnp.clip(1.0 + 0.18 * jax.random.normal(splits[7], (CS,), jnp.float32), 0.1, 1.9)
    query_weight = bell_draw(splits[8], (CS, CS), CS ** -0.5, 0.3125, ((1, 4),))
    query_bias = bell_draw(splits[9], (CS,), 0.5, 3.0, ((0, 4),), jnp.float32)
    key_weight = bell_draw(splits[10], (CS, CS), CS ** -0.5, 0.3125, ((1, 4),))
    value_weight = bell_draw(splits[11], (CS, CS), CS ** -0.5, 0.3125, ((1, 4),))
    gate_weight = bell_draw(splits[12], (CS, CS), CS ** -0.5, 0.3125, ((1, 4),))
    out_weight = bell_draw(splits[13], (CS, CS), CS ** -0.5, 0.3125, ((0, 4),))
    return dict(trunk_pair=trunk_pair, distance_bins=distance_bins, token_mask=token_mask, single=single, dist_weight=dist_weight, pair_gain=pair_gain, bias_weight=bias_weight, single_gain=single_gain, query_weight=query_weight, query_bias=query_bias, key_weight=key_weight, value_weight=value_weight, gate_weight=gate_weight, out_weight=out_weight)


def layer_norm(values, gain):
    mean = lax.optimization_barrier(jnp.mean(values, axis=-1, keepdims=True))
    centered = values - mean
    var = lax.optimization_barrier(jnp.mean(centered * centered, axis=-1, keepdims=True))
    return centered * lax.rsqrt(var + 1e-05) * gain

def reference(trunk_pair, distance_bins, token_mask, single, dist_weight, pair_gain, bias_weight, single_gain, query_weight, query_bias, key_weight, value_weight, gate_weight, out_weight):
    head_dim = CS // HEADS
    single_normed = layer_norm(single.astype(jnp.float32), single_gain.astype(jnp.float32)).astype(jnp.bfloat16)
    queries = (jnp.dot(single_normed, query_weight, preferred_element_type=jnp.float32) + query_bias).astype(jnp.bfloat16)
    keys = jnp.dot(single_normed, key_weight, preferred_element_type=jnp.float32).astype(jnp.bfloat16)
    values = jnp.dot(single_normed, value_weight, preferred_element_type=jnp.float32).astype(jnp.bfloat16)
    gate = jax.nn.sigmoid(jnp.dot(single_normed, gate_weight, preferred_element_type=jnp.float32))
    queries = queries.reshape(TOKENS, HEADS, head_dim).astype(jnp.float32)
    keys = keys.reshape(TOKENS, HEADS, head_dim).astype(jnp.float32)
    values = values.reshape(TOKENS, HEADS, head_dim).astype(jnp.float32)
    key_term = (token_mask.astype(jnp.float32) - 1.0) * 1000000000.0
    block_rows = 128
    blocks = TOKENS // block_rows
    pair_blocks = trunk_pair.reshape(blocks, block_rows, TOKENS, CZ)
    gain_pair = pair_gain.astype(jnp.float32)

    def one_sample(bins_one):

        def one_block(items):
            pair_block, bin_block = items
            onehot = (bin_block[..., None] == jnp.arange(BINS, dtype=jnp.int32)).astype(jnp.bfloat16)
            embedded = jnp.dot(onehot.reshape(-1, BINS), dist_weight, preferred_element_type=jnp.float32)
            pair_s = pair_block.astype(jnp.float32).reshape(-1, CZ) + embedded
            pair_normed = layer_norm(pair_s, gain_pair).astype(jnp.bfloat16)
            return jnp.dot(pair_normed, bias_weight, preferred_element_type=jnp.float32).astype(jnp.bfloat16).reshape(block_rows, TOKENS, HEADS)
        pair_bias = lax.map(one_block, (pair_blocks, bins_one.reshape(blocks, block_rows, TOKENS)))
        pair_bias = jnp.transpose(pair_bias.reshape(TOKENS, TOKENS, HEADS), (2, 0, 1)).astype(jnp.float32)
        scores = jnp.einsum('qhd,khd->hqk', queries, keys) / jnp.sqrt(jnp.float32(head_dim))
        scores = scores + pair_bias + key_term[None, None, :]
        probs = jax.nn.softmax(scores, axis=-1).astype(jnp.bfloat16)
        attended = jnp.einsum('hqk,khd->qhd', probs.astype(jnp.float32), values).reshape(TOKENS, CS)
        gated = (gate * attended).astype(jnp.bfloat16)
        return jnp.dot(gated, out_weight, preferred_element_type=jnp.float32).astype(jnp.bfloat16)
    return lax.map(one_sample, distance_bins)
```

```python
import functools

import jax
import jax.numpy as jnp
from jax import lax
from jax.experimental import pallas as pl
from jax.experimental.pallas import tpu as pltpu
from jax.sharding import PartitionSpec as P

F32 = jnp.float32
BF16 = jnp.bfloat16
NT = (((1,), (1,)), ((), ()))
EPS = 1e-05
VMEM = pl.BlockSpec(memory_space=pltpu.VMEM)
SMEM = pl.BlockSpec(memory_space=pltpu.SMEM)
AXES = ("sample", "row", "col")


def mm(a, b):
    return jnp.dot(a, b, preferred_element_type=F32)


def mm_nt(a, b):
    return lax.dot_general(a, b, NT, preferred_element_type=F32)


def iota(shape, dim):
    return lax.broadcasted_iota(jnp.int32, shape, dim)


def pair_kernel(
    pair_ref, bins_ref, table_ref, gain_ref, weight_ref, bias_ref, centre, table_t, gain_b
):
    rows, cols, chans = pair_ref.shape
    bins_count = table_ref.shape[0]

    @pl.when(pl.program_id(0) == 0)
    def _():
        eye = (iota((chans, chans), 0) == iota((chans, chans), 1)).astype(F32)
        centre[...] = (eye - 1.0 / chans).astype(BF16)
        table = table_ref[...].astype(F32)
        table = table - jnp.mean(table, axis=1, keepdims=True)
        high = table.astype(BF16).astype(F32)
        low = (table - high).astype(BF16).astype(F32)
        gap = jnp.zeros((48 - bins_count, chans), F32)
        tail = jnp.zeros((chans - 96, chans), F32)
        stacked = jnp.concatenate([high, gap, low, gap, tail], axis=0)
        table_t[...] = jnp.transpose(stacked)[:, :96].astype(BF16)
        gain_rows = jnp.broadcast_to(gain_ref[...], (chans, chans))
        gain_t = jnp.transpose(gain_rows)
        gain_b[...] = jnp.concatenate([gain_t] * (cols // chans), axis=1)

    weight = weight_ref[...]
    for i in range(rows):
        bins = bins_ref[pl.ds(i, 1), :]
        onehot = (iota((48, cols), 0) == bins).astype(F32).astype(BF16)
        onehot = jnp.concatenate([onehot, onehot], axis=0)
        centred = mm_nt(centre[...], pair_ref[i]) + mm(table_t[...], onehot)
        var = jnp.mean(centred * centred, axis=0, keepdims=True)
        scaled = (centred * gain_b[...]).astype(BF16)
        bias = mm(weight, scaled) * lax.rsqrt(var + EPS)
        bias_ref[i] = bias.astype(BF16)


def pair_bias(pair, bins, table, gain, weight_t, start, count, step):
    chans = pair.shape[2]
    cols = pair.shape[1]
    heads = weight_t.shape[0]
    first = start // step
    return pl.pallas_call(
        pair_kernel,
        grid=(count // step,),
        in_specs=[
            pl.BlockSpec((step, cols, chans), lambda i: (first + i, 0, 0)),
            pl.BlockSpec((step, cols), lambda i: (first + i, 0)),
            pl.BlockSpec(table.shape, lambda i: (0, 0)),
            pl.BlockSpec(gain.shape, lambda i: (0, 0)),
            pl.BlockSpec(weight_t.shape, lambda i: (0, 0)),
        ],
        out_specs=pl.BlockSpec((step, heads, cols), lambda i: (i, 0, 0)),
        out_shape=jax.ShapeDtypeStruct((count, heads, cols), BF16),
        scratch_shapes=[
            pltpu.VMEM((chans, chans), BF16),
            pltpu.VMEM((chans, 96), BF16),
            pltpu.VMEM((chans, cols), F32),
        ],
        compiler_params=pltpu.CompilerParams(vmem_limit_bytes=16 * 2**20),
        cost_estimate=pl.CostEstimate(
            flops=count * cols * 65536, bytes_accessed=count * cols * 300, transcendentals=0
        ),
        name="pair_bias",
    )(pair, bins, table, gain, weight_t)


def pack_kernel(ids, wq, wk, wv, wg, wo, qb, pay1_ref, pay2_ref, own_ref):
    core, col = ids[0], ids[1]
    group, width = wq.shape
    tiles = width // 128
    ws = (wq, wk, wv, wg)
    for w in range(4):
        for t in range(tiles):
            at = (w * tiles + t) * group
            pay1_ref[at : at + group, :] = ws[w][:, 128 * t : 128 * t + 128]
    base = 4 * tiles * group
    half = 2 * tiles * group

    @pl.when(core == 0)
    def _():
        pay2_ref[0:half, :] = pay1_ref[0:half, :]

    @pl.when(core != 0)
    def _():
        pay2_ref[0:half, :] = pay1_ref[half : 2 * half, :]

    shift = qb[...]
    high = shift.astype(BF16).astype(F32)
    low = shift - high
    lane = iota((group, 128), 1)

    def tail(dest):
        pick = (iota((width, 128), 0) - dest * group == iota((width, 128), 1)) & (
            iota((width, 128), 1) < group
        )
        cut = mm(wo[...], pick.astype(F32).astype(BF16))
        cut = jnp.where(lane == group, high, cut)
        cut = jnp.where(lane == group + 1, low, cut)
        return cut.astype(BF16)

    pay1_ref[base : base + group, :] = tail(lax.rem(col + 5 - 2 * core, 4))
    pay2_ref[half : half + group, :] = tail(lax.rem(col + 2, 4))
    own_ref[...] = tail(col)


def pack(ids, wq, wk, wv, wg, wo, qb):
    group, width = wq.shape
    tiles = width // 128
    return pl.pallas_call(
        pack_kernel,
        in_specs=[SMEM] + [VMEM] * 6,
        out_specs=[VMEM] * 3,
        out_shape=[
            jax.ShapeDtypeStruct(((4 * tiles + 1) * group, 128), BF16),
            jax.ShapeDtypeStruct(((2 * tiles + 1) * group, 128), BF16),
            jax.ShapeDtypeStruct((group, 128), BF16),
        ],
        compiler_params=pltpu.CompilerParams(vmem_limit_bytes=16 * 2**20),
        cost_estimate=pl.CostEstimate(flops=10**8, bytes_accessed=10**6, transcendentals=0),
        name="pack_weights",
    )(ids, wq, wk, wv, wg, wo, qb)


def attend_kernel(
    ids, mn, sib, wq, wk, wv, wg, own_t, p1, p2, s1, s2, gain, mask, bias_a, bias_b,
    msg_ref, gate_ref, wo_ref, x_all, w_all,
):
    core, col, ylo, rlow = ids[0], ids[1], ids[2], ids[3]
    group, width = wq.shape
    tiles = width // 128
    heads = bias_a.shape[1]
    head_dim = width // heads
    tok = 64
    keys = 256

    def place(dest, w, t, value):
        at = pl.multiple_of(dest * group, 32)
        w_all[w, pl.ds(at, group), 128 * t : 128 * t + 128] = value

    def place_tail(dest, value):
        wo_ref[pl.ds(pl.multiple_of(dest * group, 32), group), :] = value

    before, after, across = lax.rem(col + 3, 4), lax.rem(col + 1, 4), lax.rem(col + 2, 4)
    mine = jnp.where(core == 0, before, after)
    other = jnp.where(core == 0, after, before)
    own = (wq, wk, wv, wg)
    for w in range(4):
        w_all[w, pl.ds(pl.multiple_of(col * group, 32), group), :] = own[w][...]
        for t in range(tiles):
            at = (w * tiles + t) * group
            place(mine, w, t, p1[at : at + group, :])
            place(other, w, t, s1[at : at + group, :])
    for w in range(2):
        for t in range(tiles):
            at = (w * tiles + t) * group
            a, b = p2[at : at + group, :], s2[at : at + group, :]
            place(across, w, t, jnp.where(core == 0, a, b))
            place(across, w + 2, t, jnp.where(core == 0, b, a))
    base = 4 * tiles * group
    half = 2 * tiles * group
    place_tail(col, own_t[...])
    place_tail(mine, p1[base : base + group, :])
    place_tail(other, s1[base : base + group, :])
    place_tail(across, p2[half : half + group, :])

    span = mn.shape[0] // 2
    shard = mn.shape[1]
    for who, ref in ((0, mn), (1, sib)):
        for k in range(2):
            block = lax.rem(rlow + 2 * core + 2 * who + k, 4)
            rows = pl.ds(pl.multiple_of(block * tok, tok), tok)
            for q in range(2):
                at = 2 * tok * k + tok * q
                a = ref[at : at + tok, :].astype(F32)
                b = ref[span + at : span + at + tok, :].astype(F32)
                x_all[rows, shard * q : shard * q + shard] = jnp.where(ylo == 0, a, b)
                x_all[rows, shard * (q + 2) : shard * (q + 3)] = jnp.where(ylo == 0, b, a)
    at = 4 * tok
    quarters = (
        mn[at : at + tok, :].astype(F32),
        mn[span + at : span + at + tok, :].astype(F32),
        sib[at : at + tok, :].astype(F32),
        sib[span + at : span + at + tok, :].astype(F32),
    )
    here = [jnp.where(core == 0, quarters[0], quarters[2]), jnp.where(core == 0, quarters[2], quarters[0])]
    there = [jnp.where(core == 0, quarters[1], quarters[3]), jnp.where(core == 0, quarters[3], quarters[1])]
    for q in range(2):
        x_all[keys : keys + tok, shard * q : shard * q + shard] = jnp.where(ylo == 0, here[q], there[q])
        x_all[keys : keys + tok, shard * (q + 2) : shard * (q + 3)] = jnp.where(ylo == 0, there[q], here[q])

    x = x_all[...]
    centred = x - jnp.mean(x, axis=1, keepdims=True)
    var = jnp.mean(centred * centred, axis=1, keepdims=True)
    normed = (centred * lax.rsqrt(var + EPS) * gain[...]).astype(BF16)
    key_rows, query_rows = normed[:keys], normed[keys:]
    keys_all = mm_nt(key_rows, w_all[1]).astype(BF16)
    values_all = mm_nt(key_rows, w_all[2]).astype(BF16)
    lanes = iota((tok, 128), 1)
    ones = ((lanes == group) | (lanes == group + 1)).astype(F32).astype(BF16)
    queries = (mm_nt(query_rows, w_all[0]) + mm_nt(ones, wo_ref[...])).astype(BF16)
    gate_ref[...] = jax.nn.sigmoid(mm_nt(query_rows, w_all[3]))

    lane_w = iota((heads, width), 1)
    head_w = iota((heads, width), 0)
    head_mask = ((lane_w >= head_w * head_dim) & (lane_w < (head_w + 1) * head_dim)).astype(F32)
    key_term = (mask[pl.ds(col, 1), :].astype(F32) - 1.0) * 1000000000.0
    scale = 1.0 / jnp.sqrt(jnp.float32(head_dim))
    part = 16
    rows = part * heads
    spread = (iota((rows, part), 0) // heads == iota((rows, part), 1)).astype(F32).astype(BF16)
    gather = (iota((part, rows), 1) // heads == iota((part, rows), 0)).astype(F32).astype(BF16)
    lane_s = iota((rows, 128), 1)
    slot = lane_s // heads
    mine_lane = (lane_s % heads) == (iota((rows, 128), 0) % heads)
    for p in range(tok // part):
        ref = bias_a if p < 2 else bias_b
        at = part * (p % 2)
        bias = ref[at : at + part].astype(F32).reshape(rows, keys)
        wide = mm(spread, queries[part * p : part * p + part])
        wide = (wide.reshape(part, heads, width) * head_mask[None]).reshape(rows, width).astype(BF16)
        scores = mm_nt(wide, keys_all) * scale + bias + key_term
        top = jnp.max(scores, axis=1, keepdims=True)
        weights = jnp.exp(scores - top)
        total = jnp.sum(weights, axis=1, keepdims=True)
        out = mm(weights.astype(BF16), values_all) / total
        out = (out.reshape(part, heads, width) * head_mask[None]).reshape(rows, width).astype(BF16)
        t1 = top.astype(BF16).astype(F32)
        t2 = (top - t1).astype(BF16).astype(F32)
        t3 = top - t1 - t2
        l1 = total.astype(BF16).astype(F32)
        l2 = total - l1
        stats = jnp.where(slot == 0, t1, jnp.where(slot == 1, t2, jnp.where(slot == 2, t3, jnp.where(slot == 3, l1, l2))))
        stats = jnp.where(mine_lane & (slot < 5), stats, 0.0).astype(BF16)
        both = mm(gather, jnp.concatenate([out, stats], axis=1))
        msg_ref[part * p : part * p + part, :] = both.astype(BF16)


def attend(ids, mn, sib, wq, wk, wv, wg, own_t, p1, p2, s1, s2, gain, mask, bias_a, bias_b):
    group, width = wq.shape
    return pl.pallas_call(
        attend_kernel,
        in_specs=[SMEM] + [VMEM] * 15,
        out_specs=[VMEM] * 3,
        out_shape=[
            jax.ShapeDtypeStruct((64, width + 128), BF16),
            jax.ShapeDtypeStruct((64, width), F32),
            jax.ShapeDtypeStruct((width, 128), BF16),
        ],
        scratch_shapes=[
            pltpu.VMEM((320, width), F32),
            pltpu.VMEM((4, width, width), BF16),
        ],
        compiler_params=pltpu.CompilerParams(vmem_limit_bytes=24 * 2**20),
        cost_estimate=pl.CostEstimate(flops=10**9, bytes_accessed=4 * 10**6, transcendentals=300000),
        name="attend",
    )(ids, mn, sib, wq, wk, wv, wg, own_t, p1, p2, s1, s2, gain, mask, bias_a, bias_b)


def combine_kernel(m0, m1, m2, m3, gate, wo, out_ref):
    width = gate.shape[1]
    tok = m0.shape[0]
    heads = 16
    head_dim = width // heads
    lane = iota((128, width), 1)
    row = iota((128, width), 0)
    slot = row // heads
    head = row % heads
    same = (lane >= head * head_dim) & (lane < (head + 1) * head_dim)
    pick_top = (same & (slot < 3)).astype(F32).astype(BF16)
    pick_sum = (same & ((slot == 3) | (slot == 4))).astype(F32).astype(BF16)
    parts = [m0, m1, m2, m3]
    tops = [mm(m[:, width : width + 128], pick_top) for m in parts]
    sums = [mm(m[:, width : width + 128], pick_sum) for m in parts]
    best = jnp.maximum(jnp.maximum(tops[0], tops[1]), jnp.maximum(tops[2], tops[3]))
    numer = jnp.zeros((tok, width), F32)
    denom = jnp.zeros((tok, width), F32)
    for m, top, total in zip(parts, tops, sums):
        share = jnp.exp(top - best) * total
        denom = denom + share
        numer = numer + share * m[:, :width].astype(F32)
    gated = (gate[...] * (numer / denom)).astype(BF16)
    out = mm(gated, wo[...])
    out_ref[...] = out[:, : out_ref.shape[1]].astype(BF16)


def combine(m0, m1, m2, m3, gate, wo, group):
    return pl.pallas_call(
        combine_kernel,
        in_specs=[VMEM] * 6,
        out_specs=VMEM,
        out_shape=jax.ShapeDtypeStruct((m0.shape[0], group), BF16),
        compiler_params=pltpu.CompilerParams(vmem_limit_bytes=16 * 2**20),
        name="combine",
    )(m0, m1, m2, m3, gate, wo)


def device(s, r, c):
    return (s * 16 + r) * 4 + c


def long_pairs(k):
    pairs = []
    for s in range(4):
        for rb in range(4):
            for rl in range(4):
                for c in range(4):
                    source = device(s, 4 * c + (rl + 2 * (s % 2) + k) % 4, rb)
                    pairs.append((source, device(s, 4 * rb + rl, c)))
    return pairs


CORE_PAIRS = [(i, i ^ 1) for i in range(4)]
YLO_PAIRS = [(i, i ^ 2) for i in range(4)]


def side_pairs():
    return [(4 * s + c, 4 * s + (c + 1 - 2 * (s % 2)) % 4) for s in range(4) for c in range(4)]


def shift_pairs(k):
    return [(c, (c + k) % 4) for c in range(4)]


def body(
    trunk_pair, distance_bins, token_mask, single, dist_weight, pair_gain, bias_weight,
    single_gain, query_weight, query_bias, key_weight, value_weight, gate_weight, out_weight,
):
    sample = lax.axis_index("sample")
    row = lax.axis_index("row")
    col = lax.axis_index("col")
    core = sample % 2
    ids = jnp.stack([core, col, sample // 2, row % 4]).astype(jnp.int32)
    group = query_weight.shape[1]

    wq, wk, wv, wg = (w.T for w in (query_weight, key_weight, value_weight, gate_weight))
    pay1, pay2, own_t = pack(ids, wq, wk, wv, wg, out_weight, query_bias.reshape(group, 1))

    x1 = lax.ppermute(single, "sample", CORE_PAIRS)
    xa = jnp.concatenate(
        [jnp.where(core == 0, single, x1), jnp.where(core == 0, x1, single)], axis=0
    )
    a0 = lax.ppermute(xa, AXES, long_pairs(0))
    a1 = lax.ppermute(xa, AXES, long_pairs(1))
    p1 = lax.ppermute(pay1, ("sample", "col"), side_pairs())
    p2 = lax.ppermute(pay2, "col", shift_pairs(2))

    gain = pair_gain.reshape(1, -1)
    weight_t = bias_weight.T
    bins = distance_bins[0]
    bias_a = pair_bias(trunk_pair, bins, dist_weight, gain, weight_t, 0, 32, 8)

    mine = jnp.concatenate([a0, a1, single], axis=0)
    theirs = lax.ppermute(mine, "sample", YLO_PAIRS)
    bias_b = pair_bias(trunk_pair, bins, dist_weight, gain, weight_t, 32, 32, 8)
    mn = jnp.concatenate([mine, theirs], axis=0)
    sib = lax.ppermute(mn, "sample", CORE_PAIRS)
    s1 = lax.ppermute(p1, "sample", CORE_PAIRS)
    s2 = lax.ppermute(p2, "sample", CORE_PAIRS)

    msg, gate, wo = attend(
        ids, mn, sib, wq, wk, wv, wg, own_t, p1, p2, s1, s2,
        single_gain.reshape(1, -1), token_mask.reshape(4, -1), bias_a, bias_b,
    )
    others = [lax.ppermute(msg, "col", shift_pairs(k)) for k in (1, 3, 2)]
    update = combine(msg, *others, gate, wo, group)
    return update[None]


def solution(mesh):
    placed = (
        P("row", "col", None),
        P("sample", "row", "col"),
        P(),
        P("row", "sample"),
        P(),
        P(),
        P(),
        P(),
        P(None, "col"),
        P("col"),
        P(None, "col"),
        P(None, "col"),
        P(None, "col"),
        P("col", None),
    )
    return jax.shard_map(
        body, mesh=mesh, in_specs=placed, out_specs=P("sample", "row", "col"), check_vma=False
    )
```

```python
import functools

import jax
import jax.numpy as jnp
from jax import lax
from jax.experimental import pallas as pl
from jax.experimental.pallas import tpu as pltpu
from jax.sharding import PartitionSpec as P

F32 = jnp.float32
BF16 = jnp.bfloat16
NT = (((1,), (1,)), ((), ()))
EPS = 1e-05
BIG = 58 * 2**20
VMEM = pl.BlockSpec(memory_space=pltpu.VMEM)
SMEM = pl.BlockSpec(memory_space=pltpu.SMEM)
HBM = pl.BlockSpec(memory_space=pltpu.HBM)
AXES = ("sample", "row", "col")


def mm(a, b):
    return jnp.dot(a, b, preferred_element_type=F32)


def mm_nt(a, b):
    return lax.dot_general(a, b, NT, preferred_element_type=F32)


def iota(shape, dim):
    return lax.broadcasted_iota(jnp.int32, shape, dim)


def prepare_kernel(
    ids, wq, wk, wv, wg, wo, qb, single_gain, token_mask, table, pair_gain, bias_weight,
    pay1_ref, pay2_ref, own_w, own_t, centre, gain_b, weight_ref, sgain_ref, term_ref,
    wo_v, qb_v, sg_v, mask_v, table_v, pg_v, sems,
):
    core, col = ids[0], ids[1]
    group, width = wq.shape
    tiles = width // 128
    chans = table.shape[1]
    bins_count = table.shape[0]
    moves = [
        (table, table_v), (pair_gain, pg_v), (wo, wo_v), (qb, qb_v), (wq, own_w.at[0]),
        (wk, own_w.at[1]), (wv, own_w.at[2]), (wg, own_w.at[3]),
        (single_gain, sg_v), (token_mask, mask_v), (bias_weight, weight_ref),
    ]
    copies = [pltpu.make_async_copy(a, b, sems.at[i]) for i, (a, b) in enumerate(moves)]
    for c in copies:
        c.start()

    copies[0].wait()
    copies[1].wait()
    eye = (iota((chans, chans), 0) == iota((chans, chans), 1)).astype(F32)
    emb = table_v[...].astype(F32)
    emb = emb - jnp.mean(emb, axis=1, keepdims=True)
    high = emb.astype(BF16).astype(F32)
    low = emb - high
    gap = jnp.zeros((48 - bins_count, chans), F32)
    tail_rows = jnp.zeros((chans - 96, chans), F32)
    stacked = jnp.concatenate([high, gap, low, gap, tail_rows], axis=0)
    centre[...] = jnp.concatenate([eye - 1.0 / chans, jnp.transpose(stacked)], axis=1).astype(BF16)
    gain_t = jnp.transpose(jnp.broadcast_to(pg_v[...].reshape(1, chans), (chans, chans)))
    gain_b[...] = jnp.concatenate([gain_t, gain_t], axis=1)

    copies[2].wait()
    copies[3].wait()
    qb_row = jnp.concatenate([qb_v[...].reshape(1, group), jnp.zeros((1, 128 - group), F32)], axis=1)
    shift = jnp.transpose(jnp.broadcast_to(qb_row, (128, 128)))[:group]
    q_high = shift.astype(BF16).astype(F32)
    q_low = shift - q_high
    lane = iota((group, 128), 1)

    def tail(dest):
        pick = (iota((width, 128), 0) - dest * group == iota((width, 128), 1)) & (
            iota((width, 128), 1) < group
        )
        cut = mm(wo_v[...], pick.astype(F32).astype(BF16))
        cut = jnp.where(lane == group, q_high, cut)
        cut = jnp.where(lane == group + 1, q_low, cut)
        return cut.astype(BF16)

    base = 4 * tiles * group
    half = 2 * tiles * group
    pay1_ref[base : base + group, :] = tail(lax.rem(col + 5 - 2 * core, 4))
    pay2_ref[half : half + group, :] = tail(lax.rem(col + 2, 4))
    own_t[...] = tail(col)
    for c in copies[4:8]:
        c.wait()
    for w in range(4):
        for t in range(tiles):
            at = (w * tiles + t) * group
            pay1_ref[at : at + group, :] = own_w[w, :, 128 * t : 128 * t + 128]
    for w in range(2):
        for t in range(tiles):
            at = (w * tiles + t) * group
            first = own_w[w, :, 128 * t : 128 * t + 128]
            second = own_w[w + 2, :, 128 * t : 128 * t + 128]
            pay2_ref[at : at + group, :] = jnp.where(core == 0, first, second)
    for c in copies[8:]:
        c.wait()
    sgain_ref[...] = sg_v[...].reshape(1, width)
    keys = term_ref.shape[1]
    terms = (mask_v[...].astype(F32) - 1.0) * 1000000000.0
    terms = terms.reshape(1, 4 * keys)
    term = terms[:, :keys]
    for c in range(1, 4):
        term = jnp.where(col == c, terms[:, keys * c : keys * (c + 1)], term)
    term_ref[...] = term


def prepare(ids, wq, wk, wv, wg, wo, qb, single_gain, token_mask, table, pair_gain, bias_weight):
    group, width = wq.shape
    tiles = width // 128
    chans = table.shape[1]
    tokens = token_mask.shape[0]
    shape = jax.ShapeDtypeStruct
    return pl.pallas_call(
        prepare_kernel,
        in_specs=[SMEM] + [HBM] * 11,
        out_specs=[VMEM] * 9,
        out_shape=[
            shape(((4 * tiles + 1) * group, 128), BF16),
            shape(((2 * tiles + 1) * group, 128), BF16),
            shape((4, group, width), BF16),
            shape((group, 128), BF16),
            shape((chans, 2 * chans), BF16),
            shape((chans, 2 * chans), F32),
            shape(bias_weight.shape, BF16),
            shape((1, width), F32),
            shape((1, tokens // 4), F32),
        ],
        scratch_shapes=[
            pltpu.VMEM(wo.shape, BF16),
            pltpu.VMEM(qb.shape, F32),
            pltpu.VMEM(single_gain.shape, F32),
            pltpu.VMEM(token_mask.shape, jnp.int32),
            pltpu.VMEM(table.shape, BF16),
            pltpu.VMEM(pair_gain.shape, F32),
            pltpu.SemaphoreType.DMA((11,)),
        ],
        compiler_params=pltpu.CompilerParams(vmem_limit_bytes=BIG),
        name="prepare",
    )(ids, wq, wk, wv, wg, wo, qb, single_gain, token_mask, table, pair_gain, bias_weight)


def pair_rows(batch, pair_ref, pair_at, bins_ref, bins_at, centre, gain_b, weight, bias_ref, bias_at):
    cols = pair_ref.shape[1]
    sub = iota((48, cols), 0)
    pad = jnp.zeros((32, cols), BF16)
    right = []
    for i in range(batch):
        bins = bins_ref[bins_at + i : bins_at + i + 1, :]
        onehot = (sub == bins).astype(F32).astype(BF16)
        right.append(
            jnp.concatenate([jnp.transpose(pair_ref[pair_at + i]), onehot, onehot, pad], axis=0)
        )
    centred = mm(centre[...], jnp.concatenate(right, axis=1))
    var = jnp.mean(centred * centred, axis=0, keepdims=True)
    gain = jnp.concatenate([gain_b[...]] * batch, axis=1)
    bias = mm(weight[...], (centred * gain).astype(BF16)) * lax.rsqrt(var + EPS)
    for i in range(batch):
        bias_ref[bias_at + i] = bias[:, cols * i : cols * (i + 1)].astype(BF16)


def pair_kernel(start, batch, pair, bins, centre, gain_b, weight, bias_ref, buf, bins_v, centre_v, gain_v, weight_v, sems):
    rows = buf.shape[0]
    parts = rows // batch
    moves = [
        (bins.at[start : start + rows], bins_v),
        (centre, centre_v),
        (pair.at[start : start + batch], buf.at[0:batch]),
        (gain_b, gain_v),
        (weight, weight_v),
    ]
    for p in range(1, parts):
        at = batch * p
        moves.append((pair.at[start + at : start + at + batch], buf.at[at : at + batch]))
    copies = [pltpu.make_async_copy(a, b, sems.at[i]) for i, (a, b) in enumerate(moves)]
    for c in copies:
        c.start()
    for c in copies[:5]:
        c.wait()
    for p in range(parts):
        if p:
            copies[4 + p].wait()
        at = batch * p
        pair_rows(batch, buf, at, bins_v, at, centre_v, gain_v, weight_v, bias_ref, at)


def pair_bias(pair, bins, centre, gain_b, weight, start, rows, batch=8):
    cols, chans = pair.shape[1:]
    heads = weight.shape[0]
    return pl.pallas_call(
        functools.partial(pair_kernel, start, batch),
        in_specs=[HBM] * 5,
        out_specs=VMEM,
        out_shape=jax.ShapeDtypeStruct((rows, heads, cols), BF16),
        scratch_shapes=[
            pltpu.VMEM((rows, cols, chans), BF16),
            pltpu.VMEM((rows, cols), jnp.int32),
            pltpu.VMEM(centre.shape, BF16),
            pltpu.VMEM(gain_b.shape, F32),
            pltpu.VMEM(weight.shape, BF16),
            pltpu.SemaphoreType.DMA((4 + rows // batch,)),
        ],
        compiler_params=pltpu.CompilerParams(vmem_limit_bytes=BIG),
        name="pair_bias",
    )(pair, bins, centre, gain_b, weight)


def attend_kernel(
    ids, mn, sib, own_w, own_t, p1, p2, s1, s2, gain, term, bias_all,
    msg_ref, gate_ref, wo_ref, x_all, w_all,
):
    core, col, ylo, rlow = ids[0], ids[1], ids[2], ids[3]
    group, width = own_w.shape[1:]
    tiles = width // 128
    heads = bias_all.shape[1]
    head_dim = width // heads
    tok = 64
    keys = 256

    def place(dest, w, t, value):
        at = pl.multiple_of(dest * group, 32)
        w_all[w, pl.ds(at, group), 128 * t : 128 * t + 128] = value

    def place_tail(dest, value):
        wo_ref[pl.ds(pl.multiple_of(dest * group, 32), group), :] = value

    before, after, across = lax.rem(col + 3, 4), lax.rem(col + 1, 4), lax.rem(col + 2, 4)
    mine = jnp.where(core == 0, before, after)
    other = jnp.where(core == 0, after, before)
    for w in range(4):
        w_all[w, pl.ds(pl.multiple_of(col * group, 32), group), :] = own_w[w]
        for t in range(tiles):
            at = (w * tiles + t) * group
            place(mine, w, t, p1[at : at + group, :])
            place(other, w, t, s1[at : at + group, :])
    for w in range(2):
        for t in range(tiles):
            at = (w * tiles + t) * group
            a, b = p2[at : at + group, :], s2[at : at + group, :]
            place(across, w, t, jnp.where(core == 0, a, b))
            place(across, w + 2, t, jnp.where(core == 0, b, a))
    base = 4 * tiles * group
    half = 2 * tiles * group
    place_tail(col, own_t[...])
    place_tail(mine, p1[base : base + group, :])
    place_tail(other, s1[base : base + group, :])
    place_tail(across, p2[half : half + group, :])

    span = mn.shape[0] // 2
    shard = mn.shape[1]
    for who, ref in ((0, mn), (1, sib)):
        for k in range(2):
            block = lax.rem(rlow + 2 * core + 2 * who + k, 4)
            rows = pl.ds(pl.multiple_of(block * tok, tok), tok)
            at = 2 * tok * k
            near = [ref[at + tok * q : at + tok * (q + 1), :].astype(F32) for q in range(2)]
            far = [
                ref[span + at + tok * q : span + at + tok * (q + 1), :].astype(F32) for q in range(2)
            ]
            for q in range(2):
                swap = core != who
                a = jnp.where(swap, near[1 - q], near[q])
                b = jnp.where(swap, far[1 - q], far[q])
                x_all[rows, shard * q : shard * q + shard] = jnp.where(ylo == 0, a, b)
                x_all[rows, shard * (q + 2) : shard * (q + 3)] = jnp.where(ylo == 0, b, a)
    at = 4 * tok
    quarters = (
        mn[at : at + tok, :].astype(F32),
        mn[span + at : span + at + tok, :].astype(F32),
        sib[at : at + tok, :].astype(F32),
        sib[span + at : span + at + tok, :].astype(F32),
    )
    here = [jnp.where(core == 0, quarters[0], quarters[2]), jnp.where(core == 0, quarters[2], quarters[0])]
    there = [jnp.where(core == 0, quarters[1], quarters[3]), jnp.where(core == 0, quarters[3], quarters[1])]
    for q in range(2):
        x_all[keys : keys + tok, shard * q : shard * q + shard] = jnp.where(ylo == 0, here[q], there[q])
        x_all[keys : keys + tok, shard * (q + 2) : shard * (q + 3)] = jnp.where(ylo == 0, there[q], here[q])

    x = x_all[...]
    centred = x - jnp.mean(x, axis=1, keepdims=True)
    var = jnp.mean(centred * centred, axis=1, keepdims=True)
    normed = (centred * lax.rsqrt(var + EPS) * gain[...]).astype(BF16)
    key_rows, query_rows = normed[:keys], normed[keys:]
    keys_all = mm_nt(key_rows, w_all[1]).astype(BF16)
    values_all = mm_nt(key_rows, w_all[2]).astype(BF16)
    lanes = iota((tok, 128), 1)
    ones = ((lanes == group) | (lanes == group + 1)).astype(F32).astype(BF16)
    queries = (mm_nt(query_rows, w_all[0]) + mm_nt(ones, wo_ref[...])).astype(BF16)
    gate_ref[...] = jax.nn.sigmoid(mm_nt(query_rows, w_all[3]))

    lane_w = iota((heads, width), 1)
    head_w = iota((heads, width), 0)
    head_mask = ((lane_w >= head_w * head_dim) & (lane_w < (head_w + 1) * head_dim)).astype(F32)
    key_term = term[...]
    scale = 1.0 / jnp.sqrt(jnp.float32(head_dim))
    part = 16
    rows = part * heads
    spread = (iota((rows, part), 0) // heads == iota((rows, part), 1)).astype(F32).astype(BF16)
    gather = (iota((part, rows), 1) // heads == iota((part, rows), 0)).astype(F32).astype(BF16)
    lane_s = iota((rows, 128), 1)
    slot = lane_s // heads
    mine_lane = (lane_s % heads) == (iota((rows, 128), 0) % heads)
    for p in range(tok // part):
        at = part * p
        bias = bias_all[at : at + part].astype(F32).reshape(rows, keys)
        wide = mm(spread, queries[part * p : part * p + part])
        wide = (wide.reshape(part, heads, width) * head_mask[None]).reshape(rows, width).astype(BF16)
        scores = mm_nt(wide, keys_all) * scale + bias + key_term
        top = jnp.max(scores, axis=1, keepdims=True)
        weights = jnp.exp(scores - top)
        total = jnp.sum(weights, axis=1, keepdims=True)
        out = mm(weights.astype(BF16), values_all) / total
        out = (out.reshape(part, heads, width) * head_mask[None]).reshape(rows, width).astype(BF16)
        t1 = top.astype(BF16).astype(F32)
        t2 = (top - t1).astype(BF16).astype(F32)
        t3 = top - t1 - t2
        l1 = total.astype(BF16).astype(F32)
        l2 = total - l1
        stats = jnp.where(slot == 0, t1, jnp.where(slot == 1, t2, jnp.where(slot == 2, t3, jnp.where(slot == 3, l1, l2))))
        stats = jnp.where(mine_lane & (slot < 5), stats, 0.0).astype(BF16)
        both = mm(gather, jnp.concatenate([out, stats], axis=1))
        msg_ref[part * p : part * p + part, :] = both.astype(BF16)


def attend(ids, mn, sib, own_w, own_t, p1, p2, s1, s2, gain, term, bias_all):
    width = own_w.shape[2]
    return pl.pallas_call(
        attend_kernel,
        in_specs=[SMEM] + [VMEM] * 11,
        out_specs=[VMEM] * 3,
        out_shape=[
            jax.ShapeDtypeStruct((64, width + 128), BF16),
            jax.ShapeDtypeStruct((64, width), F32),
            jax.ShapeDtypeStruct((width, 128), BF16),
        ],
        scratch_shapes=[
            pltpu.VMEM((320, width), F32),
            pltpu.VMEM((4, width, width), BF16),
        ],
        compiler_params=pltpu.CompilerParams(vmem_limit_bytes=24 * 2**20),
        name="attend",
    )(ids, mn, sib, own_w, own_t, p1, p2, s1, s2, gain, term, bias_all)


def combine_kernel(m0, m1, m2, m3, gate, wo, out_ref):
    width = gate.shape[1]
    tok = m0.shape[0]
    heads = 16
    head_dim = width // heads
    lane = iota((128, width), 1)
    row = iota((128, width), 0)
    slot = row // heads
    head = row % heads
    same = (lane >= head * head_dim) & (lane < (head + 1) * head_dim)
    pick_top = (same & (slot < 3)).astype(F32).astype(BF16)
    pick_sum = (same & ((slot == 3) | (slot == 4))).astype(F32).astype(BF16)
    parts = [m0, m1, m2, m3]
    tops = [mm(m[:, width : width + 128], pick_top) for m in parts]
    sums = [mm(m[:, width : width + 128], pick_sum) for m in parts]
    best = jnp.maximum(jnp.maximum(tops[0], tops[1]), jnp.maximum(tops[2], tops[3]))
    numer = jnp.zeros((tok, width), F32)
    denom = jnp.zeros((tok, width), F32)
    for m, top, total in zip(parts, tops, sums):
        share = jnp.exp(top - best) * total
        denom = denom + share
        numer = numer + share * m[:, :width].astype(F32)
    gated = (gate[...] * (numer / denom)).astype(BF16)
    out = mm(gated, wo[...])
    out_ref[...] = out[:, : out_ref.shape[1]].astype(BF16)


def combine(m0, m1, m2, m3, gate, wo, group):
    return pl.pallas_call(
        combine_kernel,
        in_specs=[VMEM] * 6,
        out_specs=VMEM,
        out_shape=jax.ShapeDtypeStruct((m0.shape[0], group), BF16),
        compiler_params=pltpu.CompilerParams(vmem_limit_bytes=16 * 2**20),
        name="combine",
    )(m0, m1, m2, m3, gate, wo)


def device(s, r, c):
    return (s * 16 + r) * 4 + c


def long_pairs(k):
    pairs = []
    for s in range(4):
        for rb in range(4):
            for rl in range(4):
                for c in range(4):
                    source = device(s, 4 * c + (rl + 2 * (s % 2) + k) % 4, rb)
                    pairs.append((source, device(s, 4 * rb + rl, c)))
    return pairs


CORE_PAIRS = [(i, i ^ 1) for i in range(4)]
YLO_PAIRS = [(i, i ^ 2) for i in range(4)]


def side_pairs():
    return [(4 * s + c, 4 * s + (c + 1 - 2 * (s % 2)) % 4) for s in range(4) for c in range(4)]


def shift_pairs(k):
    return [(c, (c + k) % 4) for c in range(4)]


def body(
    trunk_pair, distance_bins, token_mask, single, dist_weight, pair_gain, bias_weight,
    single_gain, query_weight, query_bias, key_weight, value_weight, gate_weight, out_weight,
):
    sample = lax.axis_index("sample")
    row = lax.axis_index("row")
    col = lax.axis_index("col")
    core = sample % 2
    ids = jnp.stack([core, col, sample // 2, row % 4]).astype(jnp.int32)
    group = query_weight.shape[1]

    x1 = lax.ppermute(single, "sample", CORE_PAIRS)
    xa = jnp.concatenate([single, x1], axis=0)
    a0 = lax.ppermute(xa, AXES, long_pairs(0))
    a1 = lax.ppermute(xa, AXES, long_pairs(1))

    xa, token_mask = lax.optimization_barrier((xa, token_mask))
    wq, wk, wv, wg = (w.T for w in (query_weight, key_weight, value_weight, gate_weight))
    pay1, pay2, own_w, own_t, centre, gain_b, weight, sgain, term = prepare(
        ids, wq, wk, wv, wg, out_weight, query_bias, single_gain, token_mask,
        dist_weight, pair_gain, bias_weight.T,
    )
    p1 = lax.ppermute(pay1, ("sample", "col"), side_pairs())
    p2 = lax.ppermute(pay2, "col", shift_pairs(2))

    a0, a1, centre = lax.optimization_barrier((a0, a1, centre))
    mine = jnp.concatenate([a0, a1, single], axis=0)
    theirs = lax.ppermute(mine, "sample", YLO_PAIRS)
    bias = pair_bias(
        trunk_pair, distance_bins[0], centre, gain_b, weight, 0, trunk_pair.shape[0]
    )
    theirs, p1, p2, bias = lax.optimization_barrier((theirs, p1, p2, bias))
    mn = jnp.concatenate([mine, theirs], axis=0)
    sib = lax.ppermute(mn, "sample", CORE_PAIRS)
    s1 = lax.ppermute(p1, "sample", CORE_PAIRS)
    s2 = lax.ppermute(p2, "sample", CORE_PAIRS)

    msg, gate, wo = attend(ids, mn, sib, own_w, own_t, p1, p2, s1, s2, sgain, term, bias)
    others = [lax.ppermute(msg, "col", shift_pairs(k)) for k in (1, 3, 2)]
    update = combine(msg, *others, gate, wo, group)
    return update[None]


def solution(mesh):
    placed = (
        P("row", "col", None),
        P("sample", "row", "col"),
        P(),
        P("row", "sample"),
        P(),
        P(),
        P(),
        P(),
        P(None, "col"),
        P("col"),
        P(None, "col"),
        P(None, "col"),
        P(None, "col"),
        P("col", None),
    )
    return jax.shard_map(
        body, mesh=mesh, in_specs=placed, out_specs=P("sample", "row", "col"), check_vma=False
    )
```

```python
import functools

import jax
import jax.numpy as jnp
from jax import lax
from jax.experimental import pallas as pl
from jax.experimental.pallas import tpu as pltpu
from jax.sharding import PartitionSpec as P

F32 = jnp.float32
BF16 = jnp.bfloat16
NT = (((1,), (1,)), ((), ()))
EPS = 1e-05
BIG = 58 * 2**20
VMEM = pl.BlockSpec(memory_space=pltpu.VMEM)
HBM = pl.BlockSpec(memory_space=pltpu.HBM)
AXES = ("sample", "row", "col")


def mm(a, b):
    return jnp.dot(a, b, preferred_element_type=F32)


def mm_nt(a, b):
    return lax.dot_general(a, b, NT, preferred_element_type=F32)


def iota(shape, dim):
    return lax.broadcasted_iota(jnp.int32, shape, dim)


def prepare_kernel(
    wq, wk, wv, wg, wo, qb, single_gain, token_mask, table, pair_gain, bias_weight,
    pay1_ref, pay2_ref, own_w, own_t, centre, gain_b, weight_ref, sgain_ref, term_ref,
    wo_v, qb_v, sg_v, mask_v, table_v, pg_v, sems,
):
    core, col = lax.rem(lax.axis_index("sample"), 2), lax.axis_index("col")
    group, width = wq.shape
    tiles = width // 128
    chans = table.shape[1]
    bins_count = table.shape[0]
    moves = [
        (table, table_v), (pair_gain, pg_v), (wo, wo_v), (qb, qb_v), (wq, own_w.at[0]),
        (wk, own_w.at[1]), (wv, own_w.at[2]), (wg, own_w.at[3]),
        (single_gain, sg_v), (token_mask, mask_v), (bias_weight, weight_ref),
    ]
    copies = [pltpu.make_async_copy(a, b, sems.at[i]) for i, (a, b) in enumerate(moves)]
    for c in copies:
        c.start()

    copies[0].wait()
    copies[1].wait()
    eye = (iota((chans, chans), 0) == iota((chans, chans), 1)).astype(F32)
    emb = table_v[...].astype(F32)
    emb = emb - jnp.mean(emb, axis=1, keepdims=True)
    high = emb.astype(BF16).astype(F32)
    low = emb - high
    gap = jnp.zeros((48 - bins_count, chans), F32)
    tail_rows = jnp.zeros((chans - 96, chans), F32)
    stacked = jnp.concatenate([high, gap, low, gap, tail_rows], axis=0)
    centre[...] = jnp.concatenate([eye - 1.0 / chans, jnp.transpose(stacked)], axis=1).astype(BF16)
    gain_t = jnp.transpose(jnp.broadcast_to(pg_v[...].reshape(1, chans), (chans, chans)))
    gain_b[...] = jnp.concatenate([gain_t, gain_t], axis=1)

    copies[2].wait()
    copies[3].wait()
    qb_row = jnp.concatenate([qb_v[...].reshape(1, group), jnp.zeros((1, 128 - group), F32)], axis=1)
    shift = jnp.transpose(jnp.broadcast_to(qb_row, (128, 128)))[:group]
    q_high = shift.astype(BF16).astype(F32)
    q_low = shift - q_high
    lane = iota((group, 128), 1)

    def tail(dest):
        pick = (iota((width, 128), 0) - dest * group == iota((width, 128), 1)) & (
            iota((width, 128), 1) < group
        )
        cut = mm(wo_v[...], pick.astype(F32).astype(BF16))
        cut = jnp.where(lane == group, q_high, cut)
        cut = jnp.where(lane == group + 1, q_low, cut)
        return cut.astype(BF16)

    base = 4 * tiles * group
    half = 2 * tiles * group
    pay1_ref[base : base + group, :] = tail(lax.rem(col + 5 - 2 * core, 4))
    pay2_ref[half : half + group, :] = tail(lax.rem(col + 2, 4))
    own_t[...] = tail(col)
    for c in copies[4:8]:
        c.wait()
    for w in range(4):
        for t in range(tiles):
            at = (w * tiles + t) * group
            pay1_ref[at : at + group, :] = own_w[w, :, 128 * t : 128 * t + 128]
    for w in range(2):
        for t in range(tiles):
            at = (w * tiles + t) * group
            first = own_w[w, :, 128 * t : 128 * t + 128]
            second = own_w[w + 2, :, 128 * t : 128 * t + 128]
            pay2_ref[at : at + group, :] = jnp.where(core == 0, first, second)
    for c in copies[8:]:
        c.wait()
    sgain_ref[...] = sg_v[...].reshape(1, width)
    keys = term_ref.shape[1]
    terms = (mask_v[...].astype(F32) - 1.0) * 1000000000.0
    terms = terms.reshape(1, 4 * keys)
    term = terms[:, :keys]
    for c in range(1, 4):
        term = jnp.where(col == c, terms[:, keys * c : keys * (c + 1)], term)
    term_ref[...] = term


def prepare(wq, wk, wv, wg, wo, qb, single_gain, token_mask, table, pair_gain, bias_weight):
    group, width = wq.shape
    tiles = width // 128
    chans = table.shape[1]
    tokens = token_mask.shape[0]
    shape = jax.ShapeDtypeStruct
    return pl.pallas_call(
        prepare_kernel,
        in_specs=[HBM] * 11,
        out_specs=[VMEM] * 9,
        out_shape=[
            shape(((4 * tiles + 1) * group, 128), BF16),
            shape(((2 * tiles + 1) * group, 128), BF16),
            shape((4, group, width), BF16),
            shape((group, 128), BF16),
            shape((chans, 2 * chans), BF16),
            shape((chans, 2 * chans), F32),
            shape(bias_weight.shape, BF16),
            shape((1, width), F32),
            shape((1, tokens // 4), F32),
        ],
        scratch_shapes=[
            pltpu.VMEM(wo.shape, BF16),
            pltpu.VMEM(qb.shape, F32),
            pltpu.VMEM(single_gain.shape, F32),
            pltpu.VMEM(token_mask.shape, jnp.int32),
            pltpu.VMEM(table.shape, BF16),
            pltpu.VMEM(pair_gain.shape, F32),
            pltpu.SemaphoreType.DMA((11,)),
        ],
        compiler_params=pltpu.CompilerParams(vmem_limit_bytes=BIG),
        name="prepare",
    )(wq, wk, wv, wg, wo, qb, single_gain, token_mask, table, pair_gain, bias_weight)


def pair_rows(batch, pair_ref, pair_at, bins_ref, bins_at, centre, gain_b, weight, bias_ref, bias_at):
    cols = pair_ref.shape[1]
    sub = iota((48, cols), 0)
    pad = jnp.zeros((32, cols), BF16)
    right = []
    for i in range(batch):
        bins = bins_ref[bins_at + i : bins_at + i + 1, :]
        onehot = (sub == bins).astype(F32).astype(BF16)
        right.append(
            jnp.concatenate([jnp.transpose(pair_ref[pair_at + i]), onehot, onehot, pad], axis=0)
        )
    centred = mm(centre[...], jnp.concatenate(right, axis=1))
    var = jnp.mean(centred * centred, axis=0, keepdims=True)
    gain = jnp.concatenate([gain_b[...]] * batch, axis=1)
    bias = mm(weight[...], (centred * gain).astype(BF16)) * lax.rsqrt(var + EPS)
    for i in range(batch):
        bias_ref[bias_at + i] = bias[:, cols * i : cols * (i + 1)].astype(BF16)


def pair_kernel(batch, pair, bins, centre, gain_b, weight, bias_ref, buf, sems):
    rows = buf.shape[0]
    copies = []
    for p in range(rows // batch):
        span = pl.ds(batch * p, batch)
        copies.append(pltpu.make_async_copy(pair.at[span], buf.at[span], sems.at[p]))
    for c in copies:
        c.start()
    for p, c in enumerate(copies):
        c.wait()
        at = batch * p
        pair_rows(batch, buf, at, bins, at, centre, gain_b, weight, bias_ref, at)


def pair_bias(pair, bins, centre, gain_b, weight, batch=16):
    rows, cols, chans = pair.shape
    heads = weight.shape[0]
    return pl.pallas_call(
        functools.partial(pair_kernel, batch),
        in_specs=[HBM] + [VMEM] * 4,
        out_specs=VMEM,
        out_shape=jax.ShapeDtypeStruct((rows, heads, cols), BF16),
        scratch_shapes=[
            pltpu.VMEM((rows, cols, chans), BF16),
            pltpu.SemaphoreType.DMA((rows // batch,)),
        ],
        compiler_params=pltpu.CompilerParams(vmem_limit_bytes=53 * 2**20),
        name="pair_bias",
    )(pair, bins, centre, gain_b, weight)


def attend_kernel(
    mn, sib, own_w, own_t, p1, p2, s1, s2, gain, term, bias_all,
    msg_ref, gate_ref, wo_ref, x_all, w_all,
):
    sample = lax.axis_index("sample")
    core, ylo = lax.rem(sample, 2), sample // 2
    col = lax.axis_index("col")
    rlow = lax.rem(lax.axis_index("row"), 4)
    group, width = own_w.shape[1:]
    tiles = width // 128
    heads = bias_all.shape[1]
    head_dim = width // heads
    tok = 64
    keys = 256

    def place(dest, w, t, value):
        at = pl.multiple_of(dest * group, 32)
        w_all[w, pl.ds(at, group), 128 * t : 128 * t + 128] = value

    def place_tail(dest, value):
        wo_ref[pl.ds(pl.multiple_of(dest * group, 32), group), :] = value

    before, after, across = lax.rem(col + 3, 4), lax.rem(col + 1, 4), lax.rem(col + 2, 4)
    mine = jnp.where(core == 0, before, after)
    other = jnp.where(core == 0, after, before)
    for w in range(4):
        w_all[w, pl.ds(pl.multiple_of(col * group, 32), group), :] = own_w[w]
        for t in range(tiles):
            at = (w * tiles + t) * group
            place(mine, w, t, p1[at : at + group, :])
            place(other, w, t, s1[at : at + group, :])
    for w in range(2):
        for t in range(tiles):
            at = (w * tiles + t) * group
            a, b = p2[at : at + group, :], s2[at : at + group, :]
            place(across, w, t, jnp.where(core == 0, a, b))
            place(across, w + 2, t, jnp.where(core == 0, b, a))
    base = 4 * tiles * group
    half = 2 * tiles * group
    place_tail(col, own_t[...])
    place_tail(mine, p1[base : base + group, :])
    place_tail(other, s1[base : base + group, :])
    place_tail(across, p2[half : half + group, :])

    span = mn.shape[0] // 2
    shard = mn.shape[1]
    for who, ref in ((0, mn), (1, sib)):
        for k in range(2):
            side = core if who == 0 else 1 - core
            zlow, yhigh = rlow // 2, lax.rem(rlow, 2)
            block = 2 * lax.rem(zlow + side, 2) + lax.rem(yhigh + k, 2)
            rows = pl.ds(pl.multiple_of(block * tok, tok), tok)
            at = 2 * tok * k
            near = [ref[at + tok * q : at + tok * (q + 1), :].astype(F32) for q in range(2)]
            far = [
                ref[span + at + tok * q : span + at + tok * (q + 1), :].astype(F32) for q in range(2)
            ]
            if k == 1:
                near, far = far, near
            for q in range(2):
                swap = core != who
                a = jnp.where(swap, near[1 - q], near[q])
                b = jnp.where(swap, far[1 - q], far[q])
                x_all[rows, shard * q : shard * q + shard] = jnp.where(ylo == 0, a, b)
                x_all[rows, shard * (q + 2) : shard * (q + 3)] = jnp.where(ylo == 0, b, a)
    at = 4 * tok
    quarters = (
        mn[at : at + tok, :].astype(F32),
        mn[span + at : span + at + tok, :].astype(F32),
        sib[at : at + tok, :].astype(F32),
        sib[span + at : span + at + tok, :].astype(F32),
    )
    here = [jnp.where(core == 0, quarters[0], quarters[2]), jnp.where(core == 0, quarters[2], quarters[0])]
    there = [jnp.where(core == 0, quarters[1], quarters[3]), jnp.where(core == 0, quarters[3], quarters[1])]
    for q in range(2):
        x_all[keys : keys + tok, shard * q : shard * q + shard] = jnp.where(ylo == 0, here[q], there[q])
        x_all[keys : keys + tok, shard * (q + 2) : shard * (q + 3)] = jnp.where(ylo == 0, there[q], here[q])

    x = x_all[...]
    centred = x - jnp.mean(x, axis=1, keepdims=True)
    var = jnp.mean(centred * centred, axis=1, keepdims=True)
    normed = (centred * lax.rsqrt(var + EPS) * gain[...]).astype(BF16)
    key_rows, query_rows = normed[:keys], normed[keys:]
    keys_all = mm_nt(key_rows, w_all[1]).astype(BF16)
    values_all = mm_nt(key_rows, w_all[2]).astype(BF16)
    lanes = iota((tok, 128), 1)
    ones = ((lanes == group) | (lanes == group + 1)).astype(F32).astype(BF16)
    queries = (mm_nt(query_rows, w_all[0]) + mm_nt(ones, wo_ref[...])).astype(BF16)
    gate_ref[...] = jax.nn.sigmoid(mm_nt(query_rows, w_all[3]))

    lane_w = iota((heads, width), 1)
    head_w = iota((heads, width), 0)
    head_mask = ((lane_w >= head_w * head_dim) & (lane_w < (head_w + 1) * head_dim)).astype(F32)
    key_term = term[...]
    scale = 1.0 / jnp.sqrt(jnp.float32(head_dim))
    part = 64
    rows = part * heads
    spread = (iota((rows, part), 0) // heads == iota((rows, part), 1)).astype(F32).astype(BF16)
    gather = (iota((part, rows), 1) // heads == iota((part, rows), 0)).astype(F32).astype(BF16)
    lane_s = iota((rows, 128), 1)
    slot = lane_s // heads
    mine_lane = (lane_s % heads) == (iota((rows, 128), 0) % heads)
    for p in range(tok // part):
        at = part * p
        bias = bias_all[at : at + part].astype(F32).reshape(rows, keys)
        wide = mm(spread, queries[part * p : part * p + part])
        wide = (wide.reshape(part, heads, width) * head_mask[None]).reshape(rows, width).astype(BF16)
        scores = mm_nt(wide, keys_all) * scale + bias + key_term
        top = jnp.max(scores, axis=1, keepdims=True)
        weights = jnp.exp(scores - top)
        total = jnp.sum(weights, axis=1, keepdims=True)
        out = mm(weights.astype(BF16), values_all) * (1.0 / total)
        out = (out.reshape(part, heads, width) * head_mask[None]).reshape(rows, width).astype(BF16)
        t1 = top.astype(BF16).astype(F32)
        t2 = (top - t1).astype(BF16).astype(F32)
        t3 = top - t1 - t2
        l1 = total.astype(BF16).astype(F32)
        l2 = total - l1
        stats = jnp.where(slot == 0, t1, jnp.where(slot == 1, t2, jnp.where(slot == 2, t3, jnp.where(slot == 3, l1, l2))))
        stats = jnp.where(mine_lane & (slot < 5), stats, 0.0).astype(BF16)
        both = mm(gather, jnp.concatenate([out, stats], axis=1))
        msg_ref[part * p : part * p + part, :] = both.astype(BF16)


def attend(mn, sib, own_w, own_t, p1, p2, s1, s2, gain, term, bias_all):
    width = own_w.shape[2]
    return pl.pallas_call(
        attend_kernel,
        in_specs=[VMEM] * 11,
        out_specs=[VMEM] * 3,
        out_shape=[
            jax.ShapeDtypeStruct((64, width + 128), BF16),
            jax.ShapeDtypeStruct((64, width), F32),
            jax.ShapeDtypeStruct((width, 128), BF16),
        ],
        scratch_shapes=[
            pltpu.VMEM((320, width), F32),
            pltpu.VMEM((4, width, width), BF16),
        ],
        compiler_params=pltpu.CompilerParams(vmem_limit_bytes=24 * 2**20),
        name="attend",
    )(mn, sib, own_w, own_t, p1, p2, s1, s2, gain, term, bias_all)


def combine_kernel(m0, m1, m2, m3, gate, wo, out_ref):
    width = gate.shape[1]
    tok = m0.shape[0]
    heads = 16
    head_dim = width // heads
    lane = iota((128, width), 1)
    row = iota((128, width), 0)
    slot = row // heads
    head = row % heads
    same = (lane >= head * head_dim) & (lane < (head + 1) * head_dim)
    pick_top = (same & (slot < 3)).astype(F32).astype(BF16)
    pick_sum = (same & ((slot == 3) | (slot == 4))).astype(F32).astype(BF16)
    parts = [m0, m1, m2, m3]
    tops = [mm(m[:, width : width + 128], pick_top) for m in parts]
    sums = [mm(m[:, width : width + 128], pick_sum) for m in parts]
    best = jnp.maximum(jnp.maximum(tops[0], tops[1]), jnp.maximum(tops[2], tops[3]))
    numer = jnp.zeros((tok, width), F32)
    denom = jnp.zeros((tok, width), F32)
    for m, top, total in zip(parts, tops, sums):
        share = jnp.exp(top - best) * total
        denom = denom + share
        numer = numer + share * m[:, :width].astype(F32)
    gated = (gate[...] * (numer / denom)).astype(BF16)
    out = mm(gated, wo[...])
    out_ref[...] = out[:, : out_ref.shape[1]].astype(BF16)


def combine(m0, m1, m2, m3, gate, wo, group):
    return pl.pallas_call(
        combine_kernel,
        in_specs=[VMEM] * 6,
        out_specs=VMEM,
        out_shape=jax.ShapeDtypeStruct((m0.shape[0], group), BF16),
        compiler_params=pltpu.CompilerParams(vmem_limit_bytes=16 * 2**20),
        name="combine",
    )(m0, m1, m2, m3, gate, wo)


def device(s, r, c):
    return (s * 16 + r) * 4 + c


def long_pairs(k):
    pairs = []
    for s in range(4):
        for rb in range(4):
            for rl in range(4):
                for c in range(4):
                    near = rl ^ (2 * (s % 2)) ^ k
                    source = device(s ^ (2 * k), 4 * c + near, (rb + 2) % 4)
                    pairs.append((source, device(s, 4 * rb + rl, c)))
    return pairs


CORE_PAIRS = [(i, i ^ 1) for i in range(4)]
YLO_PAIRS = [(i, i ^ 2) for i in range(4)]


def side_pairs():
    return [(4 * s + c, 4 * s + (c + 1 - 2 * (s % 2)) % 4) for s in range(4) for c in range(4)]


def shift_pairs(k):
    return [(c, (c + k) % 4) for c in range(4)]


def body(
    trunk_pair, distance_bins, token_mask, single, dist_weight, pair_gain, bias_weight,
    single_gain, query_weight, query_bias, key_weight, value_weight, gate_weight, out_weight,
):
    group = query_weight.shape[1]

    x1 = lax.ppermute(single, "sample", CORE_PAIRS)
    xa = jnp.concatenate([single, x1], axis=0)
    a0 = lax.ppermute(xa, AXES, long_pairs(0))
    a1 = lax.ppermute(xa, AXES, long_pairs(1))

    xa, token_mask = lax.optimization_barrier((xa, token_mask))
    wq, wk, wv, wg = (w.T for w in (query_weight, key_weight, value_weight, gate_weight))
    pay1, pay2, own_w, own_t, centre, gain_b, weight, sgain, term = prepare(
        wq, wk, wv, wg, out_weight, query_bias, single_gain, token_mask,
        dist_weight, pair_gain, bias_weight.T,
    )
    a0, a1, pay1, pay2, centre = lax.optimization_barrier((a0, a1, pay1, pay2, centre))
    p1 = lax.ppermute(pay1, ("sample", "col"), side_pairs())
    p2 = lax.ppermute(pay2, "col", shift_pairs(2))

    mine = jnp.concatenate([a0, a1, xa[: single.shape[0]]], axis=0)
    theirs = lax.ppermute(mine, "sample", YLO_PAIRS)
    bias = pair_bias(trunk_pair, distance_bins[0], centre, gain_b, weight)
    theirs, p1, p2, bias = lax.optimization_barrier((theirs, p1, p2, bias))
    mn = jnp.concatenate([mine, theirs], axis=0)
    sib = lax.ppermute(mn, "sample", CORE_PAIRS)
    s1 = lax.ppermute(p1, "sample", CORE_PAIRS)
    s2 = lax.ppermute(p2, "sample", CORE_PAIRS)

    msg, gate, wo = attend(mn, sib, own_w, own_t, p1, p2, s1, s2, sgain, term, bias)
    others = [lax.ppermute(msg, "col", shift_pairs(k)) for k in (1, 3, 2)]
    update = combine(msg, *others, gate, wo, group)
    return update[None]


def solution(mesh):
    placed = (
        P("row", "col", None),
        P("sample", "row", "col"),
        P(),
        P("row", "sample"),
        P(),
        P(),
        P(),
        P(),
        P(None, "col"),
        P("col"),
        P(None, "col"),
        P(None, "col"),
        P(None, "col"),
        P("col", None),
    )
    return jax.shard_map(
        body, mesh=mesh, in_specs=placed, out_specs=P("sample", "row", "col"), check_vma=False
    )
```
